1024 devices in a mesh: ep: 32 (over z_hi, y), edp: 32 (over z_lo, x, core).
Axes of the slice: x: 8, y: 8, z: 8 (z_hi: 4, z_lo: 2; z = z_hi * 2 + z_lo), core: 2. Of those that a mesh axis runs over, the one named last changes fastest.
Arguments:
- routes: int32 [49152, 8], P(('ep', 'edp')), may hold values from 0 to 31, all different within a row; in each aligned block of 48 rows (0 to 47, 48 to 95, ...) at most 16 rows name the same one
- gate_pre: bfloat16 [32, 32, 32, 16, 768], P('ep', 'edp'), may hold values from -8 to 8
- up_pre: bfloat16 [32, 32, 32, 16, 768], P('ep', 'edp'), may hold values from -6 to 6
- hidden_grad: bfloat16 [32, 32, 32, 16, 768], P('ep', 'edp'), may hold values from -6 to 6
- w_gate: bfloat16 [32, 2048, 768], P('ep'), may hold values from -0.15625 to 0.15625
- w_up: bfloat16 [32, 2048, 768], P('ep'), may hold values from -0.15625 to 0.15625
- bucket_terms: float32 [32, 32, 128, 1536], P('ep', 'edp'), may hold values from -6 to 6
Outputs:
- token_grad: bfloat16 [49152, 2048], P(('ep', 'edp'))
- reduced: float32 [32, 128, 1536], P('ep', 'edp')
The draws below stay inside these ranges and needn't reach their ends.
Inputs may be any that keep to these rules, and one draw needn't show every extreme that they name: `routes`: each row names 8 different experts; the 48 rows of one device name no expert more than 16 times, a bound that some block reaches.
All inputs are finite; a program needn't handle non-finite values.
Results may differ from the reference program's by a relative error of at most 0.0057.
Values may be sent and summed in bfloat16 or wider, within the bound.
No kernel may reach another device: no remote copies, remote signals or barrier semaphores. Data moves between devices by JAX's collectives and lax.ppermute only.
A program may use at most 32 MiB of HBM per device.

```python
import math
import jax
import jax.numpy as jnp
import numpy as np
from jax import lax

DW = 2048
FFW = 768
TOP = 8
TOK_DEV = 48
EXPERTS = 32
CAP = 16
TOKENS = 49152
WROWS = 128
N_EP = 32
N_EDP = 32


def strengthened(array, own_key, source, target, blocks, factor):
    owner, partner = [(jnp.arange(array.shape[dim]) // (array.shape[dim] // blocks)).reshape([-1 if axis == dim else 1 for axis in range(array.ndim)]) for dim in (source, target)]
    chosen = jax.random.permutation(own_key, blocks)[partner]
    strong = (owner == chosen) | (owner == (partner + blocks // 2) % blocks)
    return jnp.where(strong, factor * array, array)


def block_scale(own_key, extent, pieces, low, high):
    level, own = 1.0, jax.random.fold_in(own_key, 6)
    for dim, blocks in pieces:
        heights = jnp.exp(jax.random.uniform(jax.random.fold_in(own, dim), (blocks,), jnp.float32, low / len(pieces), high / len(pieces)))
        level = level * jnp.repeat(heights, extent[dim] // blocks).reshape([-1 if axis == dim else 1 for axis in range(len(extent))])
    return level


def shared_out(key, own, number, rows, number_of, top, reach, slope):
    sequence = jax.random.permutation(key, number_of)
    crowded, usual = shares(number_of, rows * top, reach, slope, True), shares(number_of, rows * top, reach, slope, False)
    places = jnp.arange(number_of)

    def named(sizes, rotation):
        used = int((sizes > 0).sum())
        fixed = max(1, used // 4)
        shifted = fixed + (places - fixed + rotation * (used - fixed)) % max(1, number_of - fixed)
        return jnp.zeros((number_of,), jnp.int32).at[sequence[jnp.where(places < fixed, places, shifted)]].set(jnp.asarray(sizes, jnp.int32))

    sizes = jnp.where(number % 4 == 0, named(crowded, number // 4), named(usual, number - number // 4 - 1))
    mixed = jax.random.permutation(jax.random.fold_in(own, 3), number_of)
    giver, receiver = mixed[0:number_of // 2 * 2:2], mixed[1:number_of // 2 * 2:2]
    slack = jnp.minimum(sizes[giver] - 1, reach - sizes[receiver]) // 2
    slack = jnp.where((giver == sequence[0]) | (receiver == sequence[0]) | (sizes[receiver] == 0), 0, jnp.maximum(slack, 0))
    shifted = jax.random.randint(jax.random.fold_in(own, 4), (number_of // 2,), 0, 1 << 20) % (slack + 1)
    sizes = sizes.at[giver].add(-shifted).at[receiver].add(shifted)
    members = jnp.searchsorted(jnp.cumsum(sizes), jnp.arange(rows * top), side="right").astype(jnp.int32)
    grid = members.reshape(top, rows).T
    grid = grid[jax.random.permutation(jax.random.fold_in(own, 1), rows)]
    rotation = jax.random.randint(jax.random.fold_in(own, 2), (rows, 1), 0, top)
    return jnp.take_along_axis(grid, (jnp.arange(top)[None, :] + rotation) % top, axis=1)


def shares(number_of, total, most, lean, full):
    portions = [(1 << 20) // math.isqrt(rank ** lean) + 1 for rank in range(1, number_of + 1)]
    largest = most if full else min(most, max(-(-total // number_of), total * portions[0] // sum(portions)))
    least = 1 if total - largest >= number_of - 1 else 0
    given, rest = [largest] + [least] * (number_of - 1), total - largest - least * (number_of - 1)
    while rest > 0:
        movable = [i for i in range(1, number_of) if given[i] < largest] or [i for i in range(1, number_of) if given[i] < most]
        mass, budget = sum([portions[i] for i in movable]), rest
        for i in movable:
            extra = min(most - given[i], max(1, budget * portions[i] // mass), rest)
            given[i] = given[i] + extra
            rest = rest - extra
    return np.array(given)


def noise(key, dims, width, reach, pieces=(), held_as=jnp.bfloat16):
    drawn = width * jax.random.normal(key, dims, jnp.float32)
    if pieces:
        drawn = drawn * block_scale(key, dims, pieces, -0.22, 0.18)
    return jnp.clip(drawn, -reach, reach).astype(held_as)


def gaussian_with(own_key, dims, deviation, bound, split, heavy, kind=jnp.bfloat16):
    values = deviation * jax.random.normal(own_key, dims, jnp.float32)
    if split:
        values = values * block_scale(own_key, dims, split, -0.22, 0.18)
    return jnp.clip(strengthened(values, jax.random.fold_in(own_key, 3), *heavy), -bound, bound).astype(kind)


def setup_inputs(seed: int = 0) -> dict:
    streams_of = jax.random.split(jax.random.key(seed), 8)
    routes_keys = jax.random.split(jax.random.fold_in(streams_of[0], 1), TOKENS // TOK_DEV)
    routes_turns = jax.random.permutation(jax.random.fold_in(streams_of[0], 3), TOKENS // TOK_DEV)
    routes = jax.vmap(lambda own, number: shared_out(jax.random.fold_in(streams_of[0], 2), own, number, TOK_DEV, EXPERTS, TOP, CAP, 2))(routes_keys, routes_turns).reshape((TOKENS, TOP))
    gate_pre = noise(streams_of[1], (EXPERTS, N_EDP, N_EP, CAP, FFW), 1.5, 8.0, ((0, 32), (1, 32)))
    up_pre = noise(streams_of[2], (EXPERTS, N_EDP, N_EP, CAP, FFW), 1.0, 6.0, ((0, 32), (1, 32)))
    hidden_grad = noise(streams_of[3], (EXPERTS, N_EDP, N_EP, CAP, FFW), 1.0, 6.0, ((0, 32), (1, 32)))
    w_gate = noise(streams_of[4], (EXPERTS, DW, FFW), (2 * FFW) ** -0.5, 0.15625, ((0, 32),))
    w_up = noise(streams_of[5], (EXPERTS, DW, FFW), (2 * FFW) ** -0.5, 0.15625, ((0, 32),))
    bucket_terms = gaussian_with(streams_of[6], (N_EP, N_EDP, WROWS, 2 * FFW), 1.0, 6.0, ((0, 32), (1, 32)), (1, 2, 32, 2.75), jnp.float32)
    return dict(routes=routes, gate_pre=gate_pre, up_pre=up_pre, hidden_grad=hidden_grad, w_gate=w_gate, w_up=w_up, bucket_terms=bucket_terms)


def expert_rows(operands):
    gate_val, up_value, grad_val, gate_weight, up_weight = operands
    gate_f = gate_val.astype(jnp.float32)
    up_f = up_value.astype(jnp.float32)
    grad_f = grad_val.astype(jnp.float32)
    sigmoid_gate = 1.0 / (1.0 + jnp.exp(-gate_f))
    grad_gate = (grad_f * up_f * sigmoid_gate * (1.0 + gate_f * (1.0 - sigmoid_gate))).astype(jnp.bfloat16)
    grad_up = (grad_f * gate_f * sigmoid_gate).astype(jnp.bfloat16)
    first = jnp.dot(grad_gate.reshape(-1, FFW), gate_weight.T, preferred_element_type=jnp.float32)
    second = jnp.dot(grad_up.reshape(-1, FFW), up_weight.T, preferred_element_type=jnp.float32)
    return (first + second).astype(jnp.bfloat16).reshape(N_EDP, N_EP, CAP, DW)


def reference(routes, gate_pre, up_pre, hidden_grad, w_gate, w_up, bucket_terms):
    slot_grad = lax.map(expert_rows, (gate_pre, up_pre, hidden_grad, w_gate, w_up))
    blocks = routes.reshape(N_EP, N_EDP, TOK_DEV, TOP)
    matches = (blocks[..., None] == jnp.arange(EXPERTS, dtype=jnp.int32)).astype(jnp.int32).sum(axis=3)
    earlier = jnp.cumsum(matches, axis=2) - matches
    position = jnp.take_along_axis(earlier, blocks, axis=3)
    source = jnp.arange(N_EP, dtype=jnp.int32)[:, None, None, None]
    member = jnp.arange(N_EDP, dtype=jnp.int32)[None, :, None, None]
    rows = slot_grad[blocks, member, source, position]
    token_grad = rows.astype(jnp.float32).sum(axis=3).astype(jnp.bfloat16).reshape(TOKENS, DW)
    reduced = jnp.sum(bucket_terms, axis=1)
    return token_grad, reduced
```

```python
import jax
import jax.numpy as jnp
from jax import lax
from jax.sharding import PartitionSpec as P


def reduce_bucket(bucket):
    rows, width = bucket.shape
    members = lax.axis_size("edp")
    own = lax.axis_index("edp")
    part = bucket.reshape(members, rows * width // (members * 128), 128)
    stride = 1
    while stride < members:
        pairs = part.reshape(part.shape[0] // 2, 2, *part.shape[1:])
        bit = (own // stride) % 2
        kept = lax.dynamic_index_in_dim(pairs, bit, axis=1, keepdims=False)
        given = lax.dynamic_index_in_dim(pairs, 1 - bit, axis=1, keepdims=False)
        swap = [(i, i ^ stride) for i in range(members)]
        part = kept + lax.ppermute(given, "edp", swap)
        stride *= 2
    return part.reshape(1, rows // members, width)


def choice(routes, experts, capacity):
    matches = (routes[:, :, None] == jnp.arange(experts, dtype=jnp.int32)).any(axis=1)
    count = matches.astype(jnp.int32)
    earlier = jnp.cumsum(count, axis=0) - count
    slot = jnp.where(matches, earlier, -1)
    chosen = slot[:, :, None] == jnp.arange(capacity, dtype=jnp.int32)
    return chosen.astype(jnp.bfloat16).reshape(routes.shape[0], experts * capacity)


def shards(routes, gate_pre, up_pre, hidden_grad, w_gate, w_up, bucket_terms):
    experts = lax.axis_size("ep")
    capacity = gate_pre.shape[3]
    width, hidden = w_gate.shape[1:]
    gate_f = gate_pre.reshape(experts * capacity, hidden).astype(jnp.float32)
    up_f = up_pre.reshape(experts * capacity, hidden).astype(jnp.float32)
    grad_f = hidden_grad.reshape(experts * capacity, hidden).astype(jnp.float32)
    sigmoid_gate = 1.0 / (1.0 + jnp.exp(-gate_f))
    grad_gate = (grad_f * up_f * sigmoid_gate * (1.0 + gate_f * (1.0 - sigmoid_gate))).astype(
        jnp.bfloat16
    )
    grad_up = (grad_f * gate_f * sigmoid_gate).astype(jnp.bfloat16)
    dims = (((1,), (1,)), ((), ()))
    first = lax.dot_general(grad_gate, w_gate[0], dims, preferred_element_type=jnp.float32)
    second = lax.dot_general(grad_up, w_up[0], dims, preferred_element_type=jnp.float32)
    slot_grad = (first + second).astype(jnp.bfloat16)
    returned = lax.all_to_all(
        slot_grad.reshape(experts, capacity, width), "ep", split_axis=0, concat_axis=0, tiled=True
    )
    flat_rows = returned.reshape(experts * capacity, width)
    chosen = choice(routes, experts, capacity)
    token_grad = jnp.dot(chosen, flat_rows, preferred_element_type=jnp.float32).astype(jnp.bfloat16)
    reduced = reduce_bucket(bucket_terms[0, 0])
    return (token_grad, reduced)


def solution(mesh):
    placed = (
        P(("ep", "edp"), None),
        P("ep", "edp", None, None, None),
        P("ep", "edp", None, None, None),
        P("ep", "edp", None, None, None),
        P("ep", None, None),
        P("ep", None, None),
        P("ep", "edp", None, None),
    )
    return jax.shard_map(
        shards,
        mesh=mesh,
        in_specs=placed,
        out_specs=(P(("ep", "edp"), None), P("ep", "edp", None)),
        check_vma=False,
    )
```

```python
import jax
import jax.numpy as jnp
from jax import lax
from jax.experimental import pallas as pl
from jax.experimental.pallas import tpu as pltpu
from jax.sharding import PartitionSpec as P

BOTH = ("ep", "edp")
LINE = 8
REST = 4
TILE = 256


def reduce_bucket(bucket):
    rows, width = bucket.shape
    members = lax.axis_size("edp")
    own = lax.axis_index("edp")
    part = bucket.reshape(members, rows * width // (members * 128), 128)
    stride = 1
    while stride < members:
        pairs = part.reshape(part.shape[0] // 2, 2, *part.shape[1:])
        bit = (own // stride) % 2
        kept = lax.dynamic_index_in_dim(pairs, bit, axis=1, keepdims=False)
        given = lax.dynamic_index_in_dim(pairs, 1 - bit, axis=1, keepdims=False)
        swap = [(i, i ^ stride) for i in range(members)]
        part = kept + lax.ppermute(given, "edp", swap)
        stride *= 2
    return part.reshape(1, rows // members, width)


def place(core, member, rest):
    across = rest * LINE + member
    along = (member // 2) * LINE + rest * 2 + member % 2
    return across + core * (along - across)


def first_groups(members):
    return [
        [place(j % 2, g, r) * members + j for g in range(LINE)]
        for j in range(members)
        for r in range(REST)
    ]


def second_groups(members):
    return [
        [place(j % 2, g, r) * members + j for r in range(REST)]
        for j in range(members)
        for g in range(LINE)
    ]


def row_kernel(core_ref, gate_ref, up_ref, grad_ref, w_gate_ref, w_up_ref, out_ref, packed):
    hidden = gate_ref.shape[2]
    rows = gate_ref.shape[1]
    core = core_ref[0]

    @pl.when(pl.program_id(0) == 0)
    def _():
        def block(p, carry):
            s = place(core, p // REST, p % REST)
            gate = gate_ref[s].astype(jnp.float32)
            up = up_ref[s].astype(jnp.float32)
            grad = grad_ref[s].astype(jnp.float32)
            sig = 0.5 + 0.5 * jnp.tanh(0.5 * gate)
            scaled = grad * sig
            to = pl.ds(pl.multiple_of(p * rows, rows), rows)
            packed[to, :hidden] = (scaled * up * (1.0 + gate * (1.0 - sig))).astype(jnp.bfloat16)
            packed[to, hidden:] = (scaled * gate).astype(jnp.bfloat16)
            return carry

        lax.fori_loop(0, gate_ref.shape[0], block, 0, unroll=4)

    dims = (((1,), (1,)), ((), ()))
    total = lax.dot_general(
        packed[:, :hidden], w_gate_ref[...], dims, preferred_element_type=jnp.float32
    ) + lax.dot_general(
        packed[:, hidden:], w_up_ref[...], dims, preferred_element_type=jnp.float32
    )
    out_ref[...] = total.astype(jnp.bfloat16)


def send_rows(core, gate, up, grad, w_gate, w_up):
    sources, capacity, hidden = gate.shape
    width = w_gate.shape[0]
    whole = pl.BlockSpec((sources, capacity, hidden), lambda n, core: (0, 0, 0), pipeline_mode=pl.Buffered(1))
    weight = pl.BlockSpec((TILE, hidden), lambda n, core: (n, 0))
    return pl.pallas_call(
        row_kernel,
        grid_spec=pltpu.PrefetchScalarGridSpec(
            num_scalar_prefetch=1,
            grid=(width // TILE,),
            in_specs=[whole, whole, whole, weight, weight],
            out_specs=pl.BlockSpec((sources * capacity, TILE), lambda n, core: (0, n)),
            scratch_shapes=[pltpu.VMEM((sources * capacity, 2 * hidden), jnp.bfloat16)],
        ),
        out_shape=jax.ShapeDtypeStruct((sources * capacity, width), jnp.bfloat16),
        compiler_params=pltpu.CompilerParams(vmem_limit_bytes=60 * 1024 * 1024),
        cost_estimate=pl.CostEstimate(
            flops=4 * sources * capacity * hidden * width,
            bytes_accessed=6 * sources * capacity * hidden + 4 * hidden * width + 2 * sources * capacity * width,
            transcendentals=sources * capacity * hidden,
        ),
    )(core.reshape(1), gate, up, grad, w_gate, w_up)


def gathered_routes(routes, core, rest, experts, members):
    stack = routes[None]
    size = 1
    while size < REST:
        swap = [
            (place(j % 2, g, r) * members + j, place(j % 2, g, r ^ size) * members + j)
            for j in range(members)
            for g in range(LINE)
            for r in range(REST)
        ]
        other = lax.ppermute(stack, BOTH, swap)
        low = (rest // size) % 2 == 0
        stack = jnp.concatenate(
            [jnp.where(low, stack, other), jnp.where(low, other, stack)], axis=0
        )
        size *= 2
    return stack


def choice(routes, core, rest, capacity):
    tokens = routes.shape[1]
    named = place(core, jnp.arange(LINE, dtype=jnp.int32), rest)
    matches = (routes[:, :, :, None] == named).any(axis=2)
    count = matches.astype(jnp.int32)
    earlier = jnp.cumsum(count, axis=1) - count
    slot = jnp.where(matches, earlier, -1).reshape(REST * tokens, LINE).astype(jnp.bfloat16)
    column = jnp.arange(LINE * REST * capacity, dtype=jnp.int32)
    spread = (column[None, :] // (REST * capacity) == jnp.arange(LINE, dtype=jnp.int32)[:, None]).astype(jnp.bfloat16)
    slots = jnp.dot(slot, spread, preferred_element_type=jnp.float32)
    owner = jnp.arange(REST * tokens, dtype=jnp.int32)[:, None] // tokens
    same = owner == (column // capacity % REST)[None, :]
    chosen = same & (slots == (column % capacity).astype(jnp.float32)[None, :])
    return chosen.astype(jnp.bfloat16)


def shards(routes, gate_pre, up_pre, hidden_grad, w_gate, w_up, bucket_terms):
    members = lax.axis_size("edp")
    experts, capacity, hidden = gate_pre.shape[2:]
    tokens = routes.shape[0]
    width = w_gate.shape[1]
    core = lax.axis_index("edp") % 2
    own = lax.axis_index("ep")
    rest = jnp.where(core == 0, own // LINE, own % LINE // 2)
    rows = send_rows(core, gate_pre[0, 0], up_pre[0, 0], hidden_grad[0, 0], w_gate[0], w_up[0])
    arrived = lax.all_to_all(
        rows.reshape(LINE, REST * capacity, width),
        BOTH,
        split_axis=0,
        concat_axis=0,
        axis_index_groups=first_groups(members),
        tiled=True,
    )
    chosen = choice(gathered_routes(routes, core, rest, experts, members), core, rest, capacity)
    chosen = lax.optimization_barrier(chosen)
    partial = jnp.dot(
        chosen, arrived.reshape(experts * capacity, width), preferred_element_type=jnp.float32
    ).astype(jnp.bfloat16)
    last = lax.all_to_all(
        partial.reshape(REST, tokens, width),
        BOTH,
        split_axis=0,
        concat_axis=0,
        axis_index_groups=second_groups(members),
        tiled=True,
    )
    parts = [last[r].astype(jnp.float32) for r in range(REST)]
    token_grad = sum(parts[1:], parts[0]).astype(jnp.bfloat16)
    reduced = reduce_bucket(bucket_terms[0, 0])
    return (token_grad, reduced)


def solution(mesh):
    placed = (
        P(("ep", "edp"), None),
        P("ep", "edp", None, None, None),
        P("ep", "edp", None, None, None),
        P("ep", "edp", None, None, None),
        P("ep", None, None),
        P("ep", None, None),
        P("ep", "edp", None, None),
    )
    return jax.shard_map(
        shards,
        mesh=mesh,
        in_specs=placed,
        out_specs=(P(("ep", "edp"), None), P("ep", "edp", None)),
        check_vma=False,
    )
```

```python
import jax
import jax.numpy as jnp
from jax import lax
from jax.experimental import pallas as pl
from jax.experimental.pallas import tpu as pltpu
from jax.sharding import PartitionSpec as P

BOTH = ("ep", "edp")
GROUP = 16
CHUNKS = 4
HALVES = 2


def reduce_bucket(bucket):
    rows, width = bucket.shape
    members = lax.axis_size("edp")
    own = lax.axis_index("edp")
    part = bucket.reshape(members, rows * width // (members * 128), 128)
    stride = 1
    while stride < members:
        pairs = part.reshape(part.shape[0] // 2, 2, *part.shape[1:])
        bit = (own // stride) % 2
        kept = lax.dynamic_index_in_dim(pairs, bit, axis=1, keepdims=False)
        given = lax.dynamic_index_in_dim(pairs, 1 - bit, axis=1, keepdims=False)
        swap = [(i, i ^ stride) for i in range(members)]
        part = kept + lax.ppermute(given, "edp", swap)
        stride *= 2
    return part.reshape(1, rows // members, width)


def place(core, member, rest):
    across = rest * GROUP + member
    along = (member // 4) * 8 + rest * 4 + member % 4
    return across + core * (along - across)


def groups(members):
    return [
        [place(j % 2, g, r) * members + j for g in range(GROUP)]
        for j in range(members)
        for r in range(2)
    ]


def partners(members):
    return [
        (place(j % 2, g, r) * members + j, place(j % 2, g, 1 - r) * members + j)
        for j in range(members)
        for g in range(GROUP)
        for r in range(2)
    ]


def row_kernel(
    core_ref, gate_hbm, up_hbm, grad_hbm, w_gate_hbm, w_up_hbm, out_hbm,
    gate, up, grad, weight, packed, rows, in_sem, weight_sem, out_sem,
):
    core = core_ref[0]
    sources, capacity, hidden = gate.shape
    width = weight.shape[0]
    some, tile = sources // CHUNKS, width // HALVES
    arriving, loading, leaving = [], [], []
    for q in range(CHUNKS):
        part = pl.ds(q * some, some)
        for i, (here, there) in enumerate(((gate_hbm, gate), (up_hbm, up), (grad_hbm, grad))):
            arriving.append(pltpu.make_async_copy(here.at[part], there.at[part], in_sem.at[q, i]))
            arriving[-1].start()
    for n in range(HALVES):
        part = pl.ds(n * tile, tile)
        for i, here in enumerate((w_gate_hbm, w_up_hbm)):
            there = weight.at[part, pl.ds(i * hidden, hidden)]
            loading.append(pltpu.make_async_copy(here.at[part], there, weight_sem.at[n, i]))
            loading[-1].start()
    for q in range(CHUNKS):
        for i in range(3):
            arriving[3 * q + i].wait()
        for s in range(q * some, (q + 1) * some):
            gate_f = gate[s].astype(jnp.float32)
            up_f = up[s].astype(jnp.float32)
            grad_f = grad[s].astype(jnp.float32)
            sig = 0.5 + 0.5 * jnp.tanh(0.5 * gate_f)
            scaled = grad_f * sig
            across = s % GROUP * 2 + s // GROUP
            along = (s // 8 * 4 + s % 4) * 2 + s // 4 % 2
            position = jnp.where(core == 0, across, along)
            to = pl.ds(pl.multiple_of(position * capacity, capacity), capacity)
            packed[to, :hidden] = (scaled * up_f * (1.0 + gate_f * (1.0 - sig))).astype(jnp.bfloat16)
            packed[to, hidden:] = (scaled * gate_f).astype(jnp.bfloat16)
    for n in range(HALVES):
        part = pl.ds(n * tile, tile)
        loading[2 * n].wait()
        loading[2 * n + 1].wait()
        total = lax.dot_general(
            packed[...],
            weight[n * tile : (n + 1) * tile, :],
            (((1,), (1,)), ((), ())),
            preferred_element_type=jnp.float32,
        )
        rows[:, n * tile : (n + 1) * tile] = total.astype(jnp.bfloat16)
        leaving.append(pltpu.make_async_copy(rows.at[:, part], out_hbm.at[:, part], out_sem.at[n]))
        leaving[-1].start()
    for copy in leaving:
        copy.wait()


def send_rows(core, gate, up, grad, w_gate, w_up):
    sources, capacity, hidden = gate.shape
    width = w_gate.shape[0]
    anywhere = pl.BlockSpec(memory_space=pl.ANY)
    held = pltpu.VMEM((sources, capacity, hidden), jnp.bfloat16)
    return pl.pallas_call(
        row_kernel,
        in_specs=[pl.BlockSpec(memory_space=pltpu.SMEM)] + [anywhere] * 5,
        out_specs=anywhere,
        scratch_shapes=[
            held,
            held,
            held,
            pltpu.VMEM((width, 2 * hidden), jnp.bfloat16),
            pltpu.VMEM((sources * capacity, 2 * hidden), jnp.bfloat16),
            pltpu.VMEM((sources * capacity, width), jnp.bfloat16),
            pltpu.SemaphoreType.DMA((CHUNKS, 3)),
            pltpu.SemaphoreType.DMA((HALVES, 2)),
            pltpu.SemaphoreType.DMA((HALVES,)),
        ],
        out_shape=jax.ShapeDtypeStruct((sources * capacity, width), jnp.bfloat16),
        compiler_params=pltpu.CompilerParams(vmem_limit_bytes=60 * 1024 * 1024),
        cost_estimate=pl.CostEstimate(
            flops=4 * sources * capacity * hidden * width,
            bytes_accessed=6 * sources * capacity * hidden + 4 * hidden * width + 2 * sources * capacity * width,
            transcendentals=sources * capacity * hidden,
        ),
    )(core.reshape(1), gate, up, grad, w_gate, w_up)


def choice(routes, core, rest, capacity):
    tokens = routes.shape[1]
    named = place(core, jnp.arange(GROUP, dtype=jnp.int32), rest)
    matches = (routes[:, :, :, None] == named).any(axis=2)
    count = matches.astype(jnp.int32)
    earlier = jnp.cumsum(count, axis=1) - count
    slot = jnp.where(matches, earlier, -1).reshape(2 * tokens, GROUP).astype(jnp.bfloat16)
    column = jnp.arange(GROUP * 2 * capacity, dtype=jnp.int32)
    spread = column[None, :] // (2 * capacity) == jnp.arange(GROUP, dtype=jnp.int32)[:, None]
    slots = jnp.dot(slot, spread.astype(jnp.bfloat16), preferred_element_type=jnp.float32)
    second = jnp.arange(2 * tokens, dtype=jnp.int32)[:, None] // tokens
    owner = jnp.where(second == 0, 1 - rest, rest)
    same = owner == (column // capacity % 2)[None, :]
    chosen = same & (slots == (column % capacity).astype(jnp.float32)[None, :])
    return chosen.astype(jnp.bfloat16)


def shards(routes, gate_pre, up_pre, hidden_grad, w_gate, w_up, bucket_terms):
    members = lax.axis_size("edp")
    experts, capacity = gate_pre.shape[2:4]
    tokens = routes.shape[0]
    width = w_gate.shape[1]
    core = lax.axis_index("edp") % 2
    own = lax.axis_index("ep")
    rest = jnp.where(core == 0, own // GROUP, own // 4 % 2)
    swap = partners(members)
    rows = send_rows(core, gate_pre[0, 0], up_pre[0, 0], hidden_grad[0, 0], w_gate[0], w_up[0])
    arrived = lax.all_to_all(
        rows.reshape(GROUP, 2 * capacity, width),
        BOTH,
        split_axis=0,
        concat_axis=0,
        axis_index_groups=groups(members),
        tiled=True,
    ).reshape(experts * capacity, width)
    theirs = lax.ppermute(routes, BOTH, swap)
    chosen = choice(jnp.stack([theirs, routes]), core, rest, capacity)
    chosen = lax.optimization_barrier(chosen)
    given = jnp.dot(chosen[:tokens], arrived, preferred_element_type=jnp.float32)
    got = lax.ppermute(given.astype(jnp.bfloat16), BOTH, swap)
    kept = jnp.dot(chosen[tokens:], arrived, preferred_element_type=jnp.float32)
    token_grad = (kept + got.astype(jnp.float32)).astype(jnp.bfloat16)
    reduced = reduce_bucket(bucket_terms[0, 0])
    return (token_grad, reduced)


def solution(mesh):
    placed = (
        P(("ep", "edp"), None),
        P("ep", "edp", None, None, None),
        P("ep", "edp", None, None, None),
        P("ep", "edp", None, None, None),
        P("ep", None, None),
        P("ep", None, None),
        P("ep", "edp", None, None),
    )
    return jax.shard_map(
        shards,
        mesh=mesh,
        in_specs=placed,
        out_specs=(P(("ep", "edp"), None), P("ep", "edp", None)),
        check_vma=False,
    )
```

```python
import jax
import jax.numpy as jnp
from jax import lax
from jax.experimental import pallas as pl
from jax.experimental.pallas import tpu as pltpu
from jax.sharding import PartitionSpec as P

BOTH = ("ep", "edp")
GROUP = 16
CHUNKS = 4
HALVES = 2


def reduce_bucket(bucket):
    rows, width = bucket.shape
    members = lax.axis_size("edp")
    own = lax.axis_index("edp")
    part = bucket.reshape(members, rows * width // (members * 128), 128)
    stride = 1
    while stride < members:
        pairs = part.reshape(part.shape[0] // 2, 2, *part.shape[1:])
        bit = (own // stride) % 2
        kept = lax.dynamic_index_in_dim(pairs, bit, axis=1, keepdims=False)
        given = lax.dynamic_index_in_dim(pairs, 1 - bit, axis=1, keepdims=False)
        swap = [(i, i ^ stride) for i in range(members)]
        part = kept + lax.ppermute(given, "edp", swap)
        stride *= 2
    return part.reshape(1, rows // members, width)


def place(core, member, rest):
    across = rest * GROUP + member
    along = (member // 4) * 8 + rest * 4 + member % 4
    return across + core * (along - across)


def groups(members):
    return [
        [place(j % 2, g, r) * members + j for g in range(GROUP)]
        for j in range(members)
        for r in range(2)
    ]


def partners(members):
    return [
        (place(j % 2, g, r) * members + j, place(j % 2, g, 1 - r) * members + j)
        for j in range(members)
        for g in range(GROUP)
        for r in range(2)
    ]


def row_kernel(
    core_ref, gate_hbm, up_hbm, grad_hbm, w_gate_hbm, w_up_hbm, out_hbm,
    gate, up, grad, weight, packed, rows, in_sem, weight_sem, out_sem,
):
    core = core_ref[0]
    sources, capacity, hidden = gate.shape
    width = weight.shape[0]
    some, tile = sources // CHUNKS, width // HALVES
    arriving, loading, leaving = [], [], []
    for q in range(CHUNKS):
        part = pl.ds(q * some, some)
        for i, (here, there) in enumerate(((gate_hbm, gate), (up_hbm, up), (grad_hbm, grad))):
            arriving.append(pltpu.make_async_copy(here.at[part], there.at[part], in_sem.at[q, i]))
            arriving[-1].start()
    for n in range(HALVES):
        part = pl.ds(n * tile, tile)
        for i, here in enumerate((w_gate_hbm, w_up_hbm)):
            there = weight.at[part, pl.ds(i * hidden, hidden)]
            loading.append(pltpu.make_async_copy(here.at[part], there, weight_sem.at[n, i]))
            loading[-1].start()
    for q in range(CHUNKS):
        for i in range(3):
            arriving[3 * q + i].wait()
        for s in range(q * some, (q + 1) * some):
            gate_f = gate[s].astype(jnp.float32)
            up_f = up[s].astype(jnp.float32)
            grad_f = grad[s].astype(jnp.float32)
            sig = 0.5 + 0.5 * jnp.tanh(0.5 * gate_f)
            scaled = grad_f * sig
            across = s % GROUP * 2 + s // GROUP
            along = (s // 8 * 4 + s % 4) * 2 + s // 4 % 2
            position = jnp.where(core == 0, across, along)
            to = pl.ds(pl.multiple_of(position * capacity, capacity), capacity)
            packed[to, :hidden] = (scaled * up_f * (1.0 + gate_f * (1.0 - sig))).astype(jnp.bfloat16)
            packed[to, hidden:] = (scaled * gate_f).astype(jnp.bfloat16)
    for n in range(HALVES):
        part = pl.ds(n * tile, tile)
        loading[2 * n].wait()
        loading[2 * n + 1].wait()
        total = lax.dot_general(
            packed[...],
            weight[n * tile : (n + 1) * tile, :],
            (((1,), (1,)), ((), ())),
            preferred_element_type=jnp.float32,
        )
        rows[:, n * tile : (n + 1) * tile] = total.astype(jnp.bfloat16)
        leaving.append(pltpu.make_async_copy(rows.at[:, part], out_hbm.at[:, part], out_sem.at[n]))
        leaving[-1].start()
    for copy in leaving:
        copy.wait()


def send_rows(core, gate, up, grad, w_gate, w_up):
    sources, capacity, hidden = gate.shape
    width = w_gate.shape[0]
    anywhere = pl.BlockSpec(memory_space=pl.ANY)
    held = pltpu.VMEM((sources, capacity, hidden), jnp.bfloat16)
    return pl.pallas_call(
        row_kernel,
        in_specs=[pl.BlockSpec(memory_space=pltpu.SMEM)] + [anywhere] * 5,
        out_specs=anywhere,
        scratch_shapes=[
            held,
            held,
            held,
            pltpu.VMEM((width, 2 * hidden), jnp.bfloat16),
            pltpu.VMEM((sources * capacity, 2 * hidden), jnp.bfloat16),
            pltpu.VMEM((sources * capacity, width), jnp.bfloat16),
            pltpu.SemaphoreType.DMA((CHUNKS, 3)),
            pltpu.SemaphoreType.DMA((HALVES, 2)),
            pltpu.SemaphoreType.DMA((HALVES,)),
        ],
        out_shape=jax.ShapeDtypeStruct((sources * capacity, width), jnp.bfloat16),
        compiler_params=pltpu.CompilerParams(vmem_limit_bytes=60 * 1024 * 1024),
        cost_estimate=pl.CostEstimate(
            flops=4 * sources * capacity * hidden * width,
            bytes_accessed=6 * sources * capacity * hidden + 4 * hidden * width + 2 * sources * capacity * width,
            transcendentals=sources * capacity * hidden,
        ),
    )(core.reshape(1), gate, up, grad, w_gate, w_up)


def choice(routes, core, rest, capacity):
    tokens = routes.shape[1]
    named = place(core, jnp.arange(GROUP, dtype=jnp.int32), rest)
    matches = (routes[:, :, :, None] == named).any(axis=2)
    count = matches.astype(jnp.int32)
    earlier = jnp.cumsum(count, axis=1) - count
    slot = jnp.where(matches, earlier, -1).reshape(2 * tokens, GROUP).astype(jnp.bfloat16)
    column = jnp.arange(GROUP * 2 * capacity, dtype=jnp.int32)
    spread = column[None, :] // (2 * capacity) == jnp.arange(GROUP, dtype=jnp.int32)[:, None]
    slots = jnp.dot(slot, spread.astype(jnp.bfloat16), preferred_element_type=jnp.float32)
    second = jnp.arange(2 * tokens, dtype=jnp.int32)[:, None] // tokens
    owner = jnp.where(second == 0, 1 - rest, rest)
    same = owner == (column // capacity % 2)[None, :]
    chosen = same & (slots == (column % capacity).astype(jnp.float32)[None, :])
    return chosen.astype(jnp.bfloat16)


def shards(routes, gate_pre, up_pre, hidden_grad, w_gate, w_up, bucket_terms):
    members = lax.axis_size("edp")
    experts, capacity = gate_pre.shape[2:4]
    tokens = routes.shape[0]
    width = w_gate.shape[1]
    core = lax.axis_index("edp") % 2
    own = lax.axis_index("ep")
    rest = jnp.where(core == 0, own // GROUP, own // 4 % 2)
    swap = partners(members)
    rows = send_rows(core, gate_pre[0, 0], up_pre[0, 0], hidden_grad[0, 0], w_gate[0], w_up[0])
    theirs = lax.ppermute(routes, BOTH, swap)
    rows, theirs = lax.optimization_barrier((rows, theirs))
    arrived = lax.all_to_all(
        rows.reshape(GROUP, 2 * capacity, width),
        BOTH,
        split_axis=0,
        concat_axis=0,
        axis_index_groups=groups(members),
        tiled=True,
    ).reshape(experts * capacity, width)
    chosen = choice(jnp.stack([theirs, routes]), core, rest, capacity)
    chosen = lax.optimization_barrier(chosen)
    given = jnp.dot(chosen[:tokens], arrived, preferred_element_type=jnp.float32)
    got = lax.ppermute(given.astype(jnp.bfloat16), BOTH, swap)
    kept = jnp.dot(chosen[tokens:], arrived, preferred_element_type=jnp.float32)
    token_grad = (kept + got.astype(jnp.float32)).astype(jnp.bfloat16)
    reduced = reduce_bucket(bucket_terms[0, 0])
    return (token_grad, reduced)


def solution(mesh):
    placed = (
        P(("ep", "edp"), None),
        P("ep", "edp", None, None, None),
        P("ep", "edp", None, None, None),
        P("ep", "edp", None, None, None),
        P("ep", None, None),
        P("ep", None, None),
        P("ep", "edp", None, None),
    )
    return jax.shard_map(
        shards,
        mesh=mesh,
        in_specs=placed,
        out_specs=(P(("ep", "edp"), None), P("ep", "edp", None)),
        check_vma=False,
    )
```

```python
import jax
import jax.numpy as jnp
from jax import lax
from jax.experimental import pallas as pl
from jax.experimental.pallas import tpu as pltpu
from jax.sharding import PartitionSpec as P

BOTH = ("ep", "edp")
GROUP = 16
CHUNKS = 4
HALVES = 2


def halve(part, stride):
    members = lax.axis_size("edp")
    pairs = part.reshape(part.shape[0] // 2, 2, *part.shape[1:])
    bit = (lax.axis_index("edp") // stride) % 2
    kept = lax.dynamic_index_in_dim(pairs, bit, axis=1, keepdims=False)
    given = lax.dynamic_index_in_dim(pairs, 1 - bit, axis=1, keepdims=False)
    return kept + lax.ppermute(given, "edp", [(i, i ^ stride) for i in range(members)])


def place(core, member, rest):
    across = rest * GROUP + member
    along = (member // 4) * 8 + rest * 4 + member % 4
    return across + core * (along - across)


def groups(members):
    return [
        [place(j % 2, g, r) * members + j for g in range(GROUP)]
        for j in range(members)
        for r in range(2)
    ]


def partners(members):
    return [
        (place(j % 2, g, r) * members + j, place(j % 2, g, 1 - r) * members + j)
        for j in range(members)
        for g in range(GROUP)
        for r in range(2)
    ]


def row_kernel(
    where_ref, gate_hbm, up_hbm, grad_hbm, w_gate_hbm, w_up_hbm, out_hbm,
    gate, up, grad, weight, packed, rows, in_sem, weight_sem, out_sem,
):
    core, rest = where_ref[0], where_ref[1]
    sources, capacity, hidden = gate.shape
    width = weight.shape[0]
    some, tile = sources // CHUNKS, width // HALVES
    arriving, loading, leaving = [], [], []
    for q in range(CHUNKS):
        first = pl.ds(place(core, q * some, rest), some)
        part = pl.ds(q * some, some)
        for i, (here, there) in enumerate(((gate_hbm, gate), (up_hbm, up), (grad_hbm, grad))):
            arriving.append(pltpu.make_async_copy(here.at[first], there.at[part], in_sem.at[q, i]))
            arriving[-1].start()
    for n in range(HALVES):
        part = pl.ds(n * tile, tile)
        for i, here in enumerate((w_gate_hbm, w_up_hbm)):
            there = weight.at[part, pl.ds(i * hidden, hidden)]
            loading.append(pltpu.make_async_copy(here.at[part], there, weight_sem.at[n, i]))
            loading[-1].start()
    for q in range(CHUNKS):
        for i in range(3):
            arriving[3 * q + i].wait()
        for s in range(q * some, (q + 1) * some):
            gate_f = gate[s].astype(jnp.float32)
            up_f = up[s].astype(jnp.float32)
            grad_f = grad[s].astype(jnp.float32)
            sig = 0.5 + 0.5 * jnp.tanh(0.5 * gate_f)
            scaled = grad_f * sig
            to = pl.ds(s * capacity, capacity)
            packed[to, :hidden] = (scaled * up_f * (1.0 + gate_f * (1.0 - sig))).astype(jnp.bfloat16)
            packed[to, hidden:] = (scaled * gate_f).astype(jnp.bfloat16)
    for n in range(HALVES):
        part = pl.ds(n * tile, tile)
        loading[2 * n].wait()
        loading[2 * n + 1].wait()
        total = lax.dot_general(
            packed[...],
            weight[n * tile : (n + 1) * tile, :],
            (((1,), (1,)), ((), ())),
            preferred_element_type=jnp.float32,
        )
        rows[:, n * tile : (n + 1) * tile] = total.astype(jnp.bfloat16)
        leaving.append(pltpu.make_async_copy(rows.at[:, part], out_hbm.at[:, part], out_sem.at[n]))
        leaving[-1].start()
    for copy in leaving:
        copy.wait()


def send_rows(core, rest, gate, up, grad, w_gate, w_up):
    capacity, hidden = gate.shape[1:]
    width = w_gate.shape[0]
    anywhere = pl.BlockSpec(memory_space=pl.ANY)
    held = pltpu.VMEM((GROUP, capacity, hidden), jnp.bfloat16)
    return pl.pallas_call(
        row_kernel,
        in_specs=[pl.BlockSpec(memory_space=pltpu.SMEM)] + [anywhere] * 5,
        out_specs=anywhere,
        scratch_shapes=[
            held,
            held,
            held,
            pltpu.VMEM((width, 2 * hidden), jnp.bfloat16),
            pltpu.VMEM((GROUP * capacity, 2 * hidden), jnp.bfloat16),
            pltpu.VMEM((GROUP * capacity, width), jnp.bfloat16),
            pltpu.SemaphoreType.DMA((CHUNKS, 3)),
            pltpu.SemaphoreType.DMA((HALVES, 2)),
            pltpu.SemaphoreType.DMA((HALVES,)),
        ],
        out_shape=jax.ShapeDtypeStruct((GROUP * capacity, width), jnp.bfloat16),
        compiler_params=pltpu.CompilerParams(vmem_limit_bytes=58 * 1024 * 1024),
        cost_estimate=pl.CostEstimate(
            flops=4 * GROUP * capacity * hidden * width,
            bytes_accessed=6 * GROUP * capacity * hidden + 4 * hidden * width + 2 * GROUP * capacity * width,
            transcendentals=GROUP * capacity * hidden,
        ),
    )(jnp.stack([core, rest]), gate, up, grad, w_gate, w_up)


def choice(routes, core, rest, capacity):
    named = place(core, jnp.arange(GROUP, dtype=jnp.int32), rest)
    matches = (routes[:, :, None] == named).any(axis=1)
    count = matches.astype(jnp.int32)
    earlier = jnp.cumsum(count, axis=0) - count
    slot = jnp.where(matches, earlier, -1).astype(jnp.bfloat16)
    column = jnp.arange(GROUP * capacity, dtype=jnp.int32)
    spread = column[None, :] // capacity == jnp.arange(GROUP, dtype=jnp.int32)[:, None]
    slots = jnp.dot(slot, spread.astype(jnp.bfloat16), preferred_element_type=jnp.float32)
    return (slots == (column % capacity).astype(jnp.float32)[None, :]).astype(jnp.bfloat16)


def shards(routes, gate_pre, up_pre, hidden_grad, w_gate, w_up, bucket_terms):
    members = lax.axis_size("edp")
    capacity = gate_pre.shape[3]
    width = w_gate.shape[1]
    core = lax.axis_index("edp") % 2
    own = lax.axis_index("ep")
    rest = jnp.where(core == 0, own // GROUP, own // 4 % 2)
    swap = partners(members)
    saved = (gate_pre[0, 0], up_pre[0, 0], hidden_grad[0, 0], w_gate[0], w_up[0])

    def exchange(rows):
        return lax.all_to_all(
            rows.reshape(GROUP, capacity, width),
            BOTH,
            split_axis=0,
            concat_axis=0,
            axis_index_groups=groups(members),
            tiled=True,
        ).reshape(GROUP * capacity, width)

    theirs = lax.ppermute(routes, BOTH, swap)
    passed_on = send_rows(core, 1 - rest, *saved)
    passed_on, theirs = lax.optimization_barrier((passed_on, theirs))
    arrived = exchange(passed_on)
    own_rows = send_rows(core, rest, *saved)
    bucket = bucket_terms[0, 0]
    part = bucket.reshape(members, bucket.size // (members * 128), 128)
    part = halve(halve(part, 1), 2)
    chosen, mine, _ = lax.optimization_barrier(
        (choice(theirs, core, rest, capacity), choice(routes, core, rest, capacity), part)
    )
    given = jnp.dot(chosen, arrived, preferred_element_type=jnp.float32).astype(jnp.bfloat16)
    own_rows, given, part = lax.optimization_barrier((own_rows, given, part))
    got = lax.ppermute(given, BOTH, swap)
    kept = jnp.dot(mine, exchange(own_rows), preferred_element_type=jnp.float32)
    token_grad = (kept + got.astype(jnp.float32)).astype(jnp.bfloat16)
    part = halve(halve(halve(part, 4), 8), 16)
    reduced = part.reshape(1, bucket.shape[0] // members, bucket.shape[1])
    return (token_grad, reduced)


def solution(mesh):
    placed = (
        P(("ep", "edp"), None),
        P("ep", "edp", None, None, None),
        P("ep", "edp", None, None, None),
        P("ep", "edp", None, None, None),
        P("ep", None, None),
        P("ep", None, None),
        P("ep", "edp", None, None),
    )
    return jax.shard_map(
        shards,
        mesh=mesh,
        in_specs=placed,
        out_specs=(P(("ep", "edp"), None), P("ep", "edp", None)),
        check_vma=False,
    )
```

```python
import jax
import jax.numpy as jnp
from jax import lax
from jax.experimental import pallas as pl
from jax.experimental.pallas import tpu as pltpu
from jax.sharding import PartitionSpec as P

BOTH = ("ep", "edp")
GROUP = 16
CHUNKS = 4
HALVES = 2


def halve(part, stride, own):
    members = lax.axis_size("edp")
    pairs = part.reshape(part.shape[0] // 2, 2, *part.shape[1:])
    bit = (own // stride) % 2
    kept = lax.dynamic_index_in_dim(pairs, bit, axis=1, keepdims=False)
    given = lax.dynamic_index_in_dim(pairs, 1 - bit, axis=1, keepdims=False)
    return kept + lax.ppermute(given, "edp", [(i, i ^ stride) for i in range(members)])


def place(core, member, rest):
    across = rest * GROUP + member
    along = (member // 4) * 8 + rest * 4 + member % 4
    return across + core * (along - across)


def groups(members):
    return [
        [place(j % 2, g, r) * members + j for g in range(GROUP)]
        for j in range(members)
        for r in range(2)
    ]


def partners(members):
    return [
        (place(j % 2, g, r) * members + j, place(j % 2, g, 1 - r) * members + j)
        for j in range(members)
        for g in range(GROUP)
        for r in range(2)
    ]


def row_kernel(
    where_ref, gate_hbm, up_hbm, grad_hbm, w_gate_hbm, w_up_hbm, out_hbm,
    gate, up, grad, weight, packed, rows, in_sem, weight_sem, out_sem,
):
    core, rest = where_ref[0], where_ref[1]
    sources, capacity, hidden = gate.shape
    width = weight.shape[0]
    some, tile = sources // CHUNKS, width // HALVES
    arriving, loading, leaving = [], [], []
    for q in range(CHUNKS):
        first = pl.ds(place(core, q * some, rest), some)
        part = pl.ds(q * some, some)
        for i, (here, there) in enumerate(((gate_hbm, gate), (up_hbm, up), (grad_hbm, grad))):
            arriving.append(pltpu.make_async_copy(here.at[first], there.at[part], in_sem.at[q, i]))
            arriving[-1].start()
    for n in range(HALVES):
        part = pl.ds(n * tile, tile)
        for i, here in enumerate((w_gate_hbm, w_up_hbm)):
            there = weight.at[part, pl.ds(i * hidden, hidden)]
            loading.append(pltpu.make_async_copy(here.at[part], there, weight_sem.at[n, i]))
            loading[-1].start()
    for q in range(CHUNKS):
        for i in range(3):
            arriving[3 * q + i].wait()
        for s in range(q * some, (q + 1) * some):
            gate_f = gate[s].astype(jnp.float32)
            up_f = up[s].astype(jnp.float32)
            grad_f = grad[s].astype(jnp.float32)
            sig = 0.5 + 0.5 * jnp.tanh(0.5 * gate_f)
            scaled = grad_f * sig
            to = pl.ds(s * capacity, capacity)
            packed[to, :hidden] = (scaled * up_f * (1.0 + gate_f * (1.0 - sig))).astype(jnp.bfloat16)
            packed[to, hidden:] = (scaled * gate_f).astype(jnp.bfloat16)
    for n in range(HALVES):
        part = pl.ds(n * tile, tile)
        loading[2 * n].wait()
        loading[2 * n + 1].wait()
        total = lax.dot_general(
            packed[...],
            weight[n * tile : (n + 1) * tile, :],
            (((1,), (1,)), ((), ())),
            preferred_element_type=jnp.float32,
        )
        rows[:, n * tile : (n + 1) * tile] = total.astype(jnp.bfloat16)
        leaving.append(pltpu.make_async_copy(rows.at[:, part], out_hbm.at[:, part], out_sem.at[n]))
        leaving[-1].start()
    for copy in leaving:
        copy.wait()


def send_rows(core, rest, gate, up, grad, w_gate, w_up):
    capacity, hidden = gate.shape[1:]
    width = w_gate.shape[0]
    anywhere = pl.BlockSpec(memory_space=pl.ANY)
    held = pltpu.VMEM((GROUP, capacity, hidden), jnp.bfloat16)
    return pl.pallas_call(
        row_kernel,
        in_specs=[pl.BlockSpec(memory_space=pltpu.SMEM)] + [anywhere] * 5,
        out_specs=anywhere,
        scratch_shapes=[
            held,
            held,
            held,
            pltpu.VMEM((width, 2 * hidden), jnp.bfloat16),
            pltpu.VMEM((GROUP * capacity, 2 * hidden), jnp.bfloat16),
            pltpu.VMEM((GROUP * capacity, width), jnp.bfloat16),
            pltpu.SemaphoreType.DMA((CHUNKS, 3)),
            pltpu.SemaphoreType.DMA((HALVES, 2)),
            pltpu.SemaphoreType.DMA((HALVES,)),
        ],
        out_shape=jax.ShapeDtypeStruct((GROUP * capacity, width), jnp.bfloat16),
        compiler_params=pltpu.CompilerParams(vmem_limit_bytes=58 * 1024 * 1024),
        cost_estimate=pl.CostEstimate(
            flops=4 * GROUP * capacity * hidden * width,
            bytes_accessed=6 * GROUP * capacity * hidden + 4 * hidden * width + 2 * GROUP * capacity * width,
            transcendentals=GROUP * capacity * hidden,
        ),
    )(jnp.stack([core, rest]), gate, up, grad, w_gate, w_up)


def choice(routes, core, rest, capacity):
    named = place(core, jnp.arange(GROUP, dtype=jnp.int32), rest)
    matches = (routes[:, :, None] == named).any(axis=1)
    count = matches.astype(jnp.int32)
    earlier = jnp.cumsum(count, axis=0) - count
    slot = jnp.where(matches, earlier, -1).astype(jnp.bfloat16)
    column = jnp.arange(GROUP * capacity, dtype=jnp.int32)
    spread = column[None, :] // capacity == jnp.arange(GROUP, dtype=jnp.int32)[:, None]
    slots = jnp.dot(slot, spread.astype(jnp.bfloat16), preferred_element_type=jnp.float32)
    return (slots == (column % capacity).astype(jnp.float32)[None, :]).astype(jnp.bfloat16)


def shards(routes, gate_pre, up_pre, hidden_grad, w_gate, w_up, bucket_terms):
    members = lax.axis_size("edp")
    capacity = gate_pre.shape[3]
    width = w_gate.shape[1]
    core = lax.axis_index("edp") % 2
    own = lax.axis_index("ep")
    rest = jnp.where(core == 0, own // GROUP, own // 4 % 2)
    swap = partners(members)
    saved = (gate_pre[0, 0], up_pre[0, 0], hidden_grad[0, 0], w_gate[0], w_up[0])

    def exchange(rows):
        return lax.all_to_all(
            rows.reshape(GROUP, capacity, width),
            BOTH,
            split_axis=0,
            concat_axis=0,
            axis_index_groups=groups(members),
            tiled=True,
        ).reshape(GROUP * capacity, width)

    theirs = lax.ppermute(routes, BOTH, swap)
    passed_on = send_rows(core, 1 - rest, *saved)
    passed_on, theirs, line = lax.optimization_barrier((passed_on, theirs, lax.axis_index("edp")))
    arrived = exchange(passed_on)
    own_rows = send_rows(core, rest, *saved)
    bucket = bucket_terms[0, 0]
    part = bucket.reshape(members, bucket.size // (members * 128), 128)
    part = halve(halve(halve(part, 1, line), 2, line), 4, line)
    chosen, mine, _ = lax.optimization_barrier(
        (choice(theirs, core, rest, capacity), choice(routes, core, rest, capacity), part)
    )
    given = jnp.dot(chosen, arrived, preferred_element_type=jnp.float32).astype(jnp.bfloat16)
    own_rows, given, part = lax.optimization_barrier((own_rows, given, part))
    got = lax.ppermute(given, BOTH, swap)
    kept = jnp.dot(mine, exchange(own_rows), preferred_element_type=jnp.float32)
    token_grad = (kept + got.astype(jnp.float32)).astype(jnp.bfloat16)
    part = halve(halve(part, 8, line), 16, line)
    reduced = part.reshape(1, bucket.shape[0] // members, bucket.shape[1])
    return (token_grad, reduced)


def solution(mesh):
    placed = (
        P(("ep", "edp"), None),
        P("ep", "edp", None, None, None),
        P("ep", "edp", None, None, None),
        P("ep", "edp", None, None, None),
        P("ep", None, None),
        P("ep", None, None),
        P("ep", "edp", None, None),
    )
    return jax.shard_map(
        shards,
        mesh=mesh,
        in_specs=placed,
        out_specs=(P(("ep", "edp"), None), P("ep", "edp", None)),
        check_vma=False,
    )
```

```python
import jax
import jax.numpy as jnp
from jax import lax
from jax.experimental import pallas as pl
from jax.experimental.pallas import tpu as pltpu
from jax.sharding import PartitionSpec as P

BOTH = ("ep", "edp")
GROUP = 16
CHUNKS = 4
HALVES = 2


def place(core, member, rest):
    across = rest * GROUP + member
    along = (member // 4) * 8 + rest * 4 + member % 4
    return across + core * (along - across)


def groups(members):
    return [
        [place(j % 2, g, r) * members + j for g in range(GROUP)]
        for j in range(members)
        for r in range(2)
    ]


def partners(members):
    return [
        (place(j % 2, g, r) * members + j, place(j % 2, g, 1 - r) * members + j)
        for j in range(members)
        for g in range(GROUP)
        for r in range(2)
    ]


def row_kernel(
    core_ref, gate_hbm, up_hbm, grad_hbm, w_gate_hbm, w_up_hbm, out_hbm,
    gate, up, grad, weight, packed, rows, in_sem, weight_sem, out_sem,
):
    core = core_ref[0]
    sources, capacity, hidden = gate.shape
    width = weight.shape[0]
    some, tile = sources // CHUNKS, width // HALVES
    arriving, loading, leaving = [], [], []
    for q in range(CHUNKS):
        part = pl.ds(q * some, some)
        for i, (here, there) in enumerate(((gate_hbm, gate), (up_hbm, up), (grad_hbm, grad))):
            arriving.append(pltpu.make_async_copy(here.at[part], there.at[part], in_sem.at[q, i]))
            arriving[-1].start()
    for n in range(HALVES):
        part = pl.ds(n * tile, tile)
        for i, here in enumerate((w_gate_hbm, w_up_hbm)):
            there = weight.at[part, pl.ds(i * hidden, hidden)]
            loading.append(pltpu.make_async_copy(here.at[part], there, weight_sem.at[n, i]))
            loading[-1].start()
    for q in range(CHUNKS):
        for i in range(3):
            arriving[3 * q + i].wait()
        for s in range(q * some, (q + 1) * some):
            gate_f = gate[s].astype(jnp.float32)
            up_f = up[s].astype(jnp.float32)
            grad_f = grad[s].astype(jnp.float32)
            sig = 0.5 + 0.5 * jnp.tanh(0.5 * gate_f)
            scaled = grad_f * sig
            across = s % GROUP * 2 + s // GROUP
            along = (s // 8 * 4 + s % 4) * 2 + s // 4 % 2
            position = jnp.where(core == 0, across, along)
            to = pl.ds(pl.multiple_of(position * capacity, capacity), capacity)
            packed[to, :hidden] = (scaled * up_f * (1.0 + gate_f * (1.0 - sig))).astype(jnp.bfloat16)
            packed[to, hidden:] = (scaled * gate_f).astype(jnp.bfloat16)
    for n in range(HALVES):
        part = pl.ds(n * tile, tile)
        loading[2 * n].wait()
        loading[2 * n + 1].wait()
        total = lax.dot_general(
            packed[...],
            weight[n * tile : (n + 1) * tile, :],
            (((1,), (1,)), ((), ())),
            preferred_element_type=jnp.float32,
        )
        rows[:, n * tile : (n + 1) * tile] = total.astype(jnp.bfloat16)
        leaving.append(pltpu.make_async_copy(rows.at[:, part], out_hbm.at[:, part], out_sem.at[n]))
        leaving[-1].start()
    for copy in leaving:
        copy.wait()


def send_rows(core, gate, up, grad, w_gate, w_up):
    sources, capacity, hidden = gate.shape
    width = w_gate.shape[0]
    anywhere = pl.BlockSpec(memory_space=pl.ANY)
    held = pltpu.VMEM((sources, capacity, hidden), jnp.bfloat16)
    return pl.pallas_call(
        row_kernel,
        in_specs=[pl.BlockSpec(memory_space=pltpu.SMEM)] + [anywhere] * 5,
        out_specs=anywhere,
        scratch_shapes=[
            held,
            held,
            held,
            pltpu.VMEM((width, 2 * hidden), jnp.bfloat16),
            pltpu.VMEM((sources * capacity, 2 * hidden), jnp.bfloat16),
            pltpu.VMEM((sources * capacity, width), jnp.bfloat16),
            pltpu.SemaphoreType.DMA((CHUNKS, 3)),
            pltpu.SemaphoreType.DMA((HALVES, 2)),
            pltpu.SemaphoreType.DMA((HALVES,)),
        ],
        out_shape=jax.ShapeDtypeStruct((sources * capacity, width), jnp.bfloat16),
        compiler_params=pltpu.CompilerParams(vmem_limit_bytes=60 * 1024 * 1024),
        cost_estimate=pl.CostEstimate(
            flops=4 * sources * capacity * hidden * width,
            bytes_accessed=6 * sources * capacity * hidden + 4 * hidden * width + 2 * sources * capacity * width,
            transcendentals=sources * capacity * hidden,
        ),
    )(core.reshape(1), gate, up, grad, w_gate, w_up)


def choice(routes, core, rest, capacity):
    tokens = routes.shape[1]
    named = place(core, jnp.arange(GROUP, dtype=jnp.int32), rest)
    matches = (routes[:, :, :, None] == named).any(axis=2)
    count = matches.astype(jnp.int32)
    earlier = jnp.cumsum(count, axis=1) - count
    slot = jnp.where(matches, earlier, -1).reshape(2 * tokens, GROUP).astype(jnp.bfloat16)
    column = jnp.arange(GROUP * 2 * capacity, dtype=jnp.int32)
    spread = column[None, :] // (2 * capacity) == jnp.arange(GROUP, dtype=jnp.int32)[:, None]
    slots = jnp.dot(slot, spread.astype(jnp.bfloat16), preferred_element_type=jnp.float32)
    second = jnp.arange(2 * tokens, dtype=jnp.int32)[:, None] // tokens
    owner = jnp.where(second == 0, 1 - rest, rest)
    same = owner == (column // capacity % 2)[None, :]
    chosen = same & (slots == (column % capacity).astype(jnp.float32)[None, :])
    return chosen.astype(jnp.bfloat16)


def shards(routes, gate_pre, up_pre, hidden_grad, w_gate, w_up, bucket_terms):
    members = lax.axis_size("edp")
    experts, capacity = gate_pre.shape[2:4]
    tokens = routes.shape[0]
    width = w_gate.shape[1]
    core = lax.axis_index("edp") % 2
    own = lax.axis_index("ep")
    rest = jnp.where(core == 0, own // GROUP, own // 4 % 2)
    swap = partners(members)
    bucket = bucket_terms[0, 0]
    parts = bucket.reshape(members, bucket.size // (members * 128), 128)
    summed = lax.psum_scatter(parts, "edp", scatter_dimension=0, tiled=True)
    rows = send_rows(core, gate_pre[0, 0], up_pre[0, 0], hidden_grad[0, 0], w_gate[0], w_up[0])
    theirs = lax.ppermute(routes, BOTH, swap)
    rows, theirs = lax.optimization_barrier((rows, theirs))
    arrived = lax.all_to_all(
        rows.reshape(GROUP, 2 * capacity, width),
        BOTH,
        split_axis=0,
        concat_axis=0,
        axis_index_groups=groups(members),
        tiled=True,
    ).reshape(experts * capacity, width)
    chosen = choice(jnp.stack([theirs, routes]), core, rest, capacity)
    chosen = lax.optimization_barrier(chosen)
    given = jnp.dot(chosen[:tokens], arrived, preferred_element_type=jnp.float32)
    got = lax.ppermute(given.astype(jnp.bfloat16), BOTH, swap)
    kept = jnp.dot(chosen[tokens:], arrived, preferred_element_type=jnp.float32)
    got, kept, summed = lax.optimization_barrier((got, kept, summed))
    token_grad = (kept + got.astype(jnp.float32)).astype(jnp.bfloat16)
    reduced = summed.reshape(1, bucket.shape[0] // members, bucket.shape[1])
    return (token_grad, reduced)


def solution(mesh):
    placed = (
        P(("ep", "edp"), None),
        P("ep", "edp", None, None, None),
        P("ep", "edp", None, None, None),
        P("ep", "edp", None, None, None),
        P("ep", None, None),
        P("ep", None, None),
        P("ep", "edp", None, None),
    )
    return jax.shard_map(
        shards,
        mesh=mesh,
        in_specs=placed,
        out_specs=(P(("ep", "edp"), None), P("ep", "edp", None)),
        check_vma=False,
    )
```

```python
import jax
import jax.numpy as jnp
from jax import lax
from jax.sharding import PartitionSpec as P


def reduce_bucket(bucket):
    rows, width = bucket.shape
    members = lax.axis_size("edp")
    own = lax.axis_index("edp")
    part = bucket.reshape(members, rows * width // (members * 128), 128)
    stride = 1
    while stride < members:
        pairs = part.reshape(part.shape[0] // 2, 2, *part.shape[1:])
        bit = (own // stride) % 2
        kept = lax.dynamic_index_in_dim(pairs, bit, axis=1, keepdims=False)
        given = lax.dynamic_index_in_dim(pairs, 1 - bit, axis=1, keepdims=False)
        swap = [(i, i ^ stride) for i in range(members)]
        part = kept + lax.ppermute(given, "edp", swap)
        stride *= 2
    return part.reshape(1, rows // members, width)


def choice(routes, parity, experts, capacity):
    tokens = routes.shape[1]
    group = experts // 2
    named = 2 * jnp.arange(group, dtype=jnp.int32) + parity
    matches = (routes[:, :, :, None] == named).any(axis=2)
    count = matches.astype(jnp.int32)
    earlier = jnp.cumsum(count, axis=1) - count
    slot = jnp.where(matches, earlier, -1).reshape(2 * tokens, group).astype(jnp.bfloat16)
    column = jnp.arange(experts * capacity, dtype=jnp.int32)
    spread = column[None, :] // (2 * capacity) == jnp.arange(group, dtype=jnp.int32)[:, None]
    slots = jnp.dot(slot, spread.astype(jnp.bfloat16), preferred_element_type=jnp.float32)
    second = jnp.arange(2 * tokens, dtype=jnp.int32)[:, None] // tokens
    owner = jnp.where(second == 0, 1 - parity, parity)
    same = owner == (column // capacity % 2)[None, :]
    chosen = same & (slots == (column % capacity).astype(jnp.float32)[None, :])
    return chosen.astype(jnp.bfloat16)


def shards(routes, gate_pre, up_pre, hidden_grad, w_gate, w_up, bucket_terms):
    experts = lax.axis_size("ep")
    capacity = gate_pre.shape[3]
    tokens = routes.shape[0]
    width, hidden = w_gate.shape[1:]
    parity = lax.axis_index("ep") % 2
    swap = [(e, e ^ 1) for e in range(experts)]
    gate_f = gate_pre.reshape(experts * capacity, hidden).astype(jnp.float32)
    up_f = up_pre.reshape(experts * capacity, hidden).astype(jnp.float32)
    grad_f = hidden_grad.reshape(experts * capacity, hidden).astype(jnp.float32)
    sigmoid_gate = 0.5 + 0.5 * jnp.tanh(0.5 * gate_f)
    scaled = grad_f * sigmoid_gate
    grad_gate = (scaled * up_f * (1.0 + gate_f * (1.0 - sigmoid_gate))).astype(jnp.bfloat16)
    grad_up = (scaled * gate_f).astype(jnp.bfloat16)
    dims = (((1,), (1,)), ((), ()))
    first = lax.dot_general(grad_gate, w_gate[0], dims, preferred_element_type=jnp.float32)
    second = lax.dot_general(grad_up, w_up[0], dims, preferred_element_type=jnp.float32)
    rows = (first + second).astype(jnp.bfloat16)
    theirs = lax.ppermute(routes, "ep", swap)
    rows, theirs = lax.optimization_barrier((rows, theirs))
    arrived = lax.all_to_all(
        rows.reshape(experts // 2, 2 * capacity, width),
        "ep",
        split_axis=0,
        concat_axis=0,
        axis_index_groups=[list(range(p, experts, 2)) for p in range(2)],
        tiled=True,
    ).reshape(experts * capacity, width)
    chosen = choice(jnp.stack([theirs, routes]), parity, experts, capacity)
    chosen = lax.optimization_barrier(chosen)
    given = jnp.dot(chosen[:tokens], arrived, preferred_element_type=jnp.float32)
    got = lax.ppermute(given.astype(jnp.bfloat16), "ep", swap)
    kept = jnp.dot(chosen[tokens:], arrived, preferred_element_type=jnp.float32)
    kept = lax.optimization_barrier(kept)
    token_grad = (kept + got.astype(jnp.float32)).astype(jnp.bfloat16)
    reduced = reduce_bucket(bucket_terms[0, 0])
    return (token_grad, reduced)


def solution(mesh):
    placed = (
        P(("ep", "edp"), None),
        P("ep", "edp", None, None, None),
        P("ep", "edp", None, None, None),
        P("ep", "edp", None, None, None),
        P("ep", None, None),
        P("ep", None, None),
        P("ep", "edp", None, None),
    )
    return jax.shard_map(
        shards,
        mesh=mesh,
        in_specs=placed,
        out_specs=(P(("ep", "edp"), None), P("ep", "edp", None)),
        check_vma=False,
    )
```

```python
import jax
import jax.numpy as jnp
from jax import lax
from jax.experimental import pallas as pl
from jax.experimental.pallas import tpu as pltpu
from jax.sharding import PartitionSpec as P

CHUNKS = 4
HALVES = 2


def reduce_bucket(bucket):
    rows, width = bucket.shape
    members = lax.axis_size("edp")
    own = lax.axis_index("edp")
    part = bucket.reshape(members, rows * width // (members * 128), 128)
    stride = 1
    while stride < members:
        pairs = part.reshape(part.shape[0] // 2, 2, *part.shape[1:])
        bit = (own // stride) % 2
        kept = lax.dynamic_index_in_dim(pairs, bit, axis=1, keepdims=False)
        given = lax.dynamic_index_in_dim(pairs, 1 - bit, axis=1, keepdims=False)
        swap = [(i, i ^ stride) for i in range(members)]
        part = kept + lax.ppermute(given, "edp", swap)
        stride *= 2
    return part.reshape(1, rows // members, width)


def row_kernel(
    gate_hbm, up_hbm, grad_hbm, w_gate_hbm, w_up_hbm, out_hbm,
    gate, up, grad, weight, packed, rows, in_sem, weight_sem, out_sem,
):
    sources, capacity, hidden = gate.shape
    width = weight.shape[0]
    some, tile = sources // CHUNKS, width // HALVES
    arriving, loading, leaving = [], [], []
    for q in range(CHUNKS):
        part = pl.ds(q * some, some)
        for i, (here, there) in enumerate(((gate_hbm, gate), (up_hbm, up), (grad_hbm, grad))):
            arriving.append(pltpu.make_async_copy(here.at[part], there.at[part], in_sem.at[q, i]))
            arriving[-1].start()
    for n in range(HALVES):
        part = pl.ds(n * tile, tile)
        for i, here in enumerate((w_gate_hbm, w_up_hbm)):
            there = weight.at[part, pl.ds(i * hidden, hidden)]
            loading.append(pltpu.make_async_copy(here.at[part], there, weight_sem.at[n, i]))
            loading[-1].start()
    for q in range(CHUNKS):
        for i in range(3):
            arriving[3 * q + i].wait()
        for s in range(q * some, (q + 1) * some):
            gate_f = gate[s].astype(jnp.float32)
            up_f = up[s].astype(jnp.float32)
            grad_f = grad[s].astype(jnp.float32)
            sig = 0.5 + 0.5 * jnp.tanh(0.5 * gate_f)
            scaled = grad_f * sig
            to = pl.ds(s * capacity, capacity)
            packed[to, :hidden] = (scaled * up_f * (1.0 + gate_f * (1.0 - sig))).astype(jnp.bfloat16)
            packed[to, hidden:] = (scaled * gate_f).astype(jnp.bfloat16)
    for n in range(HALVES):
        part = pl.ds(n * tile, tile)
        loading[2 * n].wait()
        loading[2 * n + 1].wait()
        total = lax.dot_general(
            packed[...],
            weight[n * tile : (n + 1) * tile, :],
            (((1,), (1,)), ((), ())),
            preferred_element_type=jnp.float32,
        )
        rows[:, n * tile : (n + 1) * tile] = total.astype(jnp.bfloat16)
        leaving.append(pltpu.make_async_copy(rows.at[:, part], out_hbm.at[:, part], out_sem.at[n]))
        leaving[-1].start()
    for copy in leaving:
        copy.wait()


def send_rows(gate, up, grad, w_gate, w_up):
    sources, capacity, hidden = gate.shape
    width = w_gate.shape[0]
    anywhere = pl.BlockSpec(memory_space=pl.ANY)
    held = pltpu.VMEM((sources, capacity, hidden), jnp.bfloat16)
    return pl.pallas_call(
        row_kernel,
        in_specs=[anywhere] * 5,
        out_specs=anywhere,
        scratch_shapes=[
            held,
            held,
            held,
            pltpu.VMEM((width, 2 * hidden), jnp.bfloat16),
            pltpu.VMEM((sources * capacity, 2 * hidden), jnp.bfloat16),
            pltpu.VMEM((sources * capacity, width), jnp.bfloat16),
            pltpu.SemaphoreType.DMA((CHUNKS, 3)),
            pltpu.SemaphoreType.DMA((HALVES, 2)),
            pltpu.SemaphoreType.DMA((HALVES,)),
        ],
        out_shape=jax.ShapeDtypeStruct((sources * capacity, width), jnp.bfloat16),
        compiler_params=pltpu.CompilerParams(vmem_limit_bytes=60 * 1024 * 1024),
        cost_estimate=pl.CostEstimate(
            flops=4 * sources * capacity * hidden * width,
            bytes_accessed=6 * sources * capacity * hidden + 4 * hidden * width + 2 * sources * capacity * width,
            transcendentals=sources * capacity * hidden,
        ),
    )(gate, up, grad, w_gate, w_up)


def choice(routes, experts, capacity):
    named = jnp.arange(experts, dtype=jnp.int32)
    matches = (routes[:, :, None] == named).any(axis=1)
    count = matches.astype(jnp.int32)
    earlier = jnp.cumsum(count, axis=0) - count
    slot = jnp.where(matches, earlier, -1).astype(jnp.bfloat16)
    column = jnp.arange(experts * capacity, dtype=jnp.int32)
    spread = column[None, :] // capacity == named[:, None]
    slots = jnp.dot(slot, spread.astype(jnp.bfloat16), preferred_element_type=jnp.float32)
    return (slots == (column % capacity).astype(jnp.float32)[None, :]).astype(jnp.bfloat16)


def shards(routes, gate_pre, up_pre, hidden_grad, w_gate, w_up, bucket_terms):
    experts, capacity = gate_pre.shape[2:4]
    width = w_gate.shape[1]
    rows = send_rows(gate_pre[0, 0], up_pre[0, 0], hidden_grad[0, 0], w_gate[0], w_up[0])
    arrived = lax.all_to_all(
        rows.reshape(experts, capacity, width), "ep", split_axis=0, concat_axis=0, tiled=True
    ).reshape(experts * capacity, width)
    chosen = lax.optimization_barrier(choice(routes, experts, capacity))
    token_grad = jnp.dot(chosen, arrived, preferred_element_type=jnp.float32).astype(jnp.bfloat16)
    reduced = reduce_bucket(bucket_terms[0, 0])
    return (token_grad, reduced)


def solution(mesh):
    placed = (
        P(("ep", "edp"), None),
        P("ep", "edp", None, None, None),
        P("ep", "edp", None, None, None),
        P("ep", "edp", None, None, None),
        P("ep", None, None),
        P("ep", None, None),
        P("ep", "edp", None, None),
    )
    return jax.shard_map(
        shards,
        mesh=mesh,
        in_specs=placed,
        out_specs=(P(("ep", "edp"), None), P("ep", "edp", None)),
        check_vma=False,
    )
```

```python
import jax
import jax.numpy as jnp
from jax import lax
from jax.experimental import pallas as pl
from jax.experimental.pallas import tpu as pltpu
from jax.sharding import PartitionSpec as P

BOTH = ("ep", "edp")
GROUP = 16
CHUNKS = 4
HALVES = 2


def reduce_bucket(bucket):
    rows, width = bucket.shape
    members = lax.axis_size("edp")
    own = lax.axis_index("edp")
    part = bucket.reshape(members, rows * width // (members * 128), 128)
    stride = 1
    while stride < members:
        pairs = part.reshape(part.shape[0] // 2, 2, *part.shape[1:])
        bit = (own // stride) % 2
        kept = lax.dynamic_index_in_dim(pairs, bit, axis=1, keepdims=False)
        given = lax.dynamic_index_in_dim(pairs, 1 - bit, axis=1, keepdims=False)
        swap = [(i, i ^ stride) for i in range(members)]
        part = kept + lax.ppermute(given, "edp", swap)
        stride *= 2
    return part.reshape(1, rows // members, width)


def place(core, member, rest):
    across = rest * GROUP + member
    along = (member // 4) * 8 + rest * 4 + member % 4
    return across + core * (along - across)


def groups(members):
    return [
        [place(j % 2, g, r) * members + j for g in range(GROUP)]
        for j in range(members)
        for r in range(2)
    ]


def partners(members):
    return [
        (place(j % 2, g, r) * members + j, place(j % 2, g, 1 - r) * members + j)
        for j in range(members)
        for g in range(GROUP)
        for r in range(2)
    ]


def row_kernel(
    core_ref, gate_hbm, up_hbm, grad_hbm, w_gate_hbm, w_up_hbm, out_hbm,
    gate, up, grad, weight, packed, rows, in_sem, weight_sem, out_sem,
):
    core = core_ref[0]
    sources, capacity, hidden = gate.shape
    width = weight.shape[0]
    some, tile = sources // CHUNKS, width // HALVES
    arriving, loading, leaving = [], [], []
    for q in range(CHUNKS):
        part = pl.ds(q * some, some)
        for i, (here, there) in enumerate(((gate_hbm, gate), (up_hbm, up), (grad_hbm, grad))):
            arriving.append(pltpu.make_async_copy(here.at[part], there.at[part], in_sem.at[q, i]))
            arriving[-1].start()
    for n in range(HALVES):
        part = pl.ds(n * tile, tile)
        for i, here in enumerate((w_gate_hbm, w_up_hbm)):
            there = weight.at[part, pl.ds(i * hidden, hidden)]
            loading.append(pltpu.make_async_copy(here.at[part], there, weight_sem.at[n, i]))
            loading[-1].start()
    for q in range(CHUNKS):
        for i in range(3):
            arriving[3 * q + i].wait()
        for s in range(q * some, (q + 1) * some):
            gate_f = gate[s].astype(jnp.float32)
            up_f = up[s].astype(jnp.float32)
            grad_f = grad[s].astype(jnp.float32)
            sig = 0.5 + 0.5 * jnp.tanh(0.5 * gate_f)
            scaled = grad_f * sig
            across = s % GROUP * 2 + s // GROUP
            along = (s // 8 * 4 + s % 4) * 2 + s // 4 % 2
            position = jnp.where(core == 0, across, along)
            to = pl.ds(pl.multiple_of(position * capacity, capacity), capacity)
            packed[to, :hidden] = (scaled * up_f * (1.0 + gate_f * (1.0 - sig))).astype(jnp.bfloat16)
            packed[to, hidden:] = (scaled * gate_f).astype(jnp.bfloat16)
    for n in range(HALVES):
        part = pl.ds(n * tile, tile)
        loading[2 * n].wait()
        loading[2 * n + 1].wait()
        total = lax.dot_general(
            packed[...],
            weight[n * tile : (n + 1) * tile, :],
            (((1,), (1,)), ((), ())),
            preferred_element_type=jnp.float32,
        )
        rows[:, n * tile : (n + 1) * tile] = total.astype(jnp.bfloat16)
        leaving.append(pltpu.make_async_copy(rows.at[:, part], out_hbm.at[:, part], out_sem.at[n]))
        leaving[-1].start()
    for copy in leaving:
        copy.wait()


def send_rows(core, gate, up, grad, w_gate, w_up):
    sources, capacity, hidden = gate.shape
    width = w_gate.shape[0]
    anywhere = pl.BlockSpec(memory_space=pl.ANY)
    held = pltpu.VMEM((sources, capacity, hidden), jnp.bfloat16)
    return pl.pallas_call(
        row_kernel,
        in_specs=[pl.BlockSpec(memory_space=pltpu.SMEM)] + [anywhere] * 5,
        out_specs=anywhere,
        scratch_shapes=[
            held,
            held,
            held,
            pltpu.VMEM((width, 2 * hidden), jnp.bfloat16),
            pltpu.VMEM((sources * capacity, 2 * hidden), jnp.bfloat16),
            pltpu.VMEM((sources * capacity, width), jnp.bfloat16),
            pltpu.SemaphoreType.DMA((CHUNKS, 3)),
            pltpu.SemaphoreType.DMA((HALVES, 2)),
            pltpu.SemaphoreType.DMA((HALVES,)),
        ],
        out_shape=jax.ShapeDtypeStruct((sources * capacity, width), jnp.bfloat16),
        compiler_params=pltpu.CompilerParams(vmem_limit_bytes=60 * 1024 * 1024),
        cost_estimate=pl.CostEstimate(
            flops=4 * sources * capacity * hidden * width,
            bytes_accessed=6 * sources * capacity * hidden + 4 * hidden * width + 2 * sources * capacity * width,
            transcendentals=sources * capacity * hidden,
        ),
    )(core.reshape(1), gate, up, grad, w_gate, w_up)


def choice(routes, core, rest, capacity):
    tokens = routes.shape[1]
    named = place(core, jnp.arange(GROUP, dtype=jnp.int32), rest)
    matches = (routes[:, :, :, None] == named).any(axis=2)
    count = matches.astype(jnp.int32)
    earlier = jnp.cumsum(count, axis=1) - count
    slot = jnp.where(matches, earlier, -1).reshape(2 * tokens, GROUP).astype(jnp.bfloat16)
    column = jnp.arange(GROUP * 2 * capacity, dtype=jnp.int32)
    spread = column[None, :] // (2 * capacity) == jnp.arange(GROUP, dtype=jnp.int32)[:, None]
    slots = jnp.dot(slot, spread.astype(jnp.bfloat16), preferred_element_type=jnp.float32)
    second = jnp.arange(2 * tokens, dtype=jnp.int32)[:, None] // tokens
    owner = jnp.where(second == 0, 1 - rest, rest)
    same = owner == (column // capacity % 2)[None, :]
    chosen = same & (slots == (column % capacity).astype(jnp.float32)[None, :])
    return chosen.astype(jnp.bfloat16)


def shards(routes, gate_pre, up_pre, hidden_grad, w_gate, w_up, bucket_terms):
    members = lax.axis_size("edp")
    experts, capacity = gate_pre.shape[2:4]
    tokens = routes.shape[0]
    width = w_gate.shape[1]
    core = lax.axis_index("edp") % 2
    own = lax.axis_index("ep")
    rest = jnp.where(core == 0, own // GROUP, own // 4 % 2)
    swap = partners(members)
    rows = send_rows(core, gate_pre[0, 0], up_pre[0, 0], hidden_grad[0, 0], w_gate[0], w_up[0])
    theirs = lax.ppermute(routes, BOTH, swap)
    rows, theirs = lax.optimization_barrier((rows, theirs))
    arrived = lax.all_to_all(
        rows.reshape(GROUP, 2 * capacity, width),
        BOTH,
        split_axis=0,
        concat_axis=0,
        axis_index_groups=groups(members),
        tiled=True,
    ).reshape(experts * capacity, width)
    chosen = choice(jnp.stack([theirs, routes]), core, rest, capacity)
    chosen = lax.optimization_barrier(chosen)
    given = jnp.dot(chosen[:tokens], arrived, preferred_element_type=jnp.float32)
    got = lax.ppermute(given.astype(jnp.bfloat16), BOTH, swap)
    kept = jnp.dot(chosen[tokens:], arrived, preferred_element_type=jnp.float32)
    kept = lax.optimization_barrier(kept)
    token_grad = (kept + got.astype(jnp.float32)).astype(jnp.bfloat16)
    reduced = reduce_bucket(bucket_terms[0, 0])
    return (token_grad, reduced)


def solution(mesh):
    placed = (
        P(("ep", "edp"), None),
        P("ep", "edp", None, None, None),
        P("ep", "edp", None, None, None),
        P("ep", "edp", None, None, None),
        P("ep", None, None),
        P("ep", None, None),
        P("ep", "edp", None, None),
    )
    return jax.shard_map(
        shards,
        mesh=mesh,
        in_specs=placed,
        out_specs=(P(("ep", "edp"), None), P("ep", "edp", None)),
        check_vma=False,
    )
```
